128 devices in a mesh: dyn: 64 (over x, y, z), grp: 2 (over core).
Axes of the slice: x: 4, y: 4, z: 4, core: 2. Of those that a mesh axis runs over, the one named last changes fastest.
Arguments:
- fields: float32 [16, 72, 32768], P(None, None, ('dyn', 'grp')), may hold values from -6 to 6
- velocity: float32 [2, 16, 72, 32768], P(None, None, None, ('dyn', 'grp')), may hold values from -1 to 1
- neighbors: int32 [4, 32768], P(None, ('dyn', 'grp')), may hold values from 0 to 32767, as said below
- column_slot: int32 [16, 32768], P(None, ('dyn', 'grp')), may hold values from 0 to 524287, as said below
- surface: bfloat16 [16, 524288], P(None, 'dyn'), may hold values from -6 to 6
- w_profile: bfloat16 [72, 1024], replicated, may hold values from -0.625 to 0.625
- w_surface: bfloat16 [16, 1024], replicated, may hold values from -0.625 to 0.625
- b_first: float32 [1024], replicated, may hold values from -4 to 4
- w_second: bfloat16 [1024, 1024], replicated, may hold values from -0.1875 to 0.1875
- b_second: float32 [1024], replicated, may hold values from -4 to 4
- w_third: bfloat16 [1024, 1024], replicated, may hold values from -0.1875 to 0.1875
- b_third: float32 [1024], replicated, may hold values from -4 to 4
- w_out: bfloat16 [1024, 72], replicated, may hold values from -0.1875 to 0.1875
- b_out: float32 [72], replicated, may hold values from -3 to 3
Outputs:
- advanced_state: float32 [16, 72, 32768], P(None, None, ('dyn', 'grp'))
- heating: bfloat16 [16, 72, 32768], P(None, None, ('dyn', 'grp'))
The draws below stay inside these ranges and needn't reach their ends.
Inputs may be any that keep to these rules, and one draw needn't show every extreme that they name: neighbors[k, e] = (e + o) mod 32768 with 1 <= |o| <= 32; |o| = 32 occurs. `column_slot`: all slots are distinct. With e // 256 = 2 d + g, every column (n, e) gets slot b * 2 * 4096 + g * 4096 + d * 64 + k with 0 <= k < 64; each pair of source and block b gets exactly 64 columns.
All inputs are finite; a program needn't handle non-finite values.
Results may differ from the reference program's by a relative error of at most 0.0053.
Values may be sent and summed in bfloat16 or wider, within the bound.
No kernel may reach another device: no remote copies, remote signals or barrier semaphores. Data moves between devices by JAX's collectives and lax.ppermute only.
A program may use at most 192 MiB of HBM per device.

```python
import math
import jax
import jax.numpy as jnp
import numpy as np
from jax import lax

NODES = 16
LEV = 72
HID = 1024
NAUX = 16
STEPS = 4
REACH = 32
ELEMENTS = 32768
COLS_DEV = 4096
PEER = 64
COLUMNS = 524288
N_DYN = 64
N_GRP = 2


def draw_neighbors(key, part):
    key = jax.random.fold_in(key, 11)
    first_key, second_key = jax.random.split(key)
    magnitude = jax.random.randint(first_key, (4, ELEMENTS), 1, REACH + 1)
    direction = jax.random.randint(second_key, (4, ELEMENTS), 0, 2) * 2 - 1
    offset = (magnitude * direction).at[0, 0].set(REACH)
    return ((jnp.arange(ELEMENTS)[None, :] + offset) % ELEMENTS).astype(jnp.int32)


def shuffle_one(sub_key):
    return jax.random.permutation(sub_key, COLS_DEV)


def draw_column_slot(key, part):
    key = jax.random.fold_in(key, 23)
    sources = N_DYN * N_GRP
    key_list = jax.random.split(key, sources)
    order = jax.vmap(shuffle_one)(key_list)
    source_ids = jnp.arange(sources)[:, None]
    rank = jnp.zeros((sources, COLS_DEV), jnp.int32).at[source_ids, order].set(jnp.arange(COLS_DEV, dtype=jnp.int32)[None, :])
    dyn_index = source_ids // N_GRP
    grp_index = source_ids % N_GRP
    block_index = rank // PEER
    within = rank % PEER
    slots_all = block_index * (2 * COLS_DEV) + grp_index * COLS_DEV + dyn_index * PEER + within
    return jnp.transpose(slots_all.reshape(ELEMENTS, NODES)).astype(jnp.int32)


def level_of(stream_key, dims, cuts, least, high):
    factor_of, own = 1.0, jax.random.fold_in(stream_key, 6)
    for dim, shards_of in cuts:
        steps = jnp.exp(jax.random.uniform(jax.random.fold_in(own, dim), (shards_of,), jnp.float32, least / len(cuts), high / len(cuts)))
        factor_of = factor_of * jnp.repeat(steps, dims[dim] // shards_of).reshape([-1 if axis == dim else 1 for axis in range(len(dims))])
    return factor_of


def scatter_about(stream_key, dims, deviation, bound, cuts=(), kind=jnp.bfloat16):
    factor_of = level_of(stream_key, dims, cuts, -0.22, 0.18) if cuts else 1.0
    drawn = jax.random.normal(stream_key, dims, jnp.float32) * deviation * factor_of
    return jnp.minimum(jnp.maximum(drawn, -bound), bound).astype(kind)


def setup_inputs(seed: int = 0) -> dict:
    streams_of = jax.random.split(jax.random.key(seed), 15)
    return {
        "fields": scatter_about(streams_of[0], (NODES, LEV, ELEMENTS), 1.0, 6.0, ((2, 128),), jnp.float32),
        "velocity": jnp.clip(jax.random.uniform(streams_of[1], (2, NODES, LEV, ELEMENTS), jnp.float32, -1.0, 1.0) * level_of(streams_of[1], (2, NODES, LEV, ELEMENTS), ((3, 128),), -0.4, 0.0), -1.0, 1.0),
        "neighbors": draw_neighbors(jax.random.fold_in(streams_of[14], 71), 0),
        "column_slot": draw_column_slot(jax.random.fold_in(streams_of[14], 71), 0),
        "surface": scatter_about(streams_of[4], (NAUX, COLUMNS), 1.0, 6.0, ((1, 64),)),
        "w_profile": scatter_about(streams_of[5], (LEV, HID), (LEV + NAUX) ** -0.5, 0.625),
        "w_surface": scatter_about(streams_of[6], (NAUX, HID), (LEV + NAUX) ** -0.5, 0.625),
        "b_first": scatter_about(streams_of[7], (HID,), 1.0, 4.0, (), jnp.float32),
        "w_second": scatter_about(streams_of[8], (HID, HID), HID ** -0.5, 0.1875),
        "b_second": scatter_about(streams_of[9], (HID,), 1.0, 4.0, (), jnp.float32),
        "w_third": scatter_about(streams_of[10], (HID, HID), HID ** -0.5, 0.1875),
        "b_third": scatter_about(streams_of[11], (HID,), 1.0, 4.0, (), jnp.float32),
        "w_out": scatter_about(streams_of[12], (HID, LEV), HID ** -0.5, 0.1875),
        "b_out": scatter_about(streams_of[13], (LEV,), 0.5, 3.0, (), jnp.float32),
    }


step_size = 0.05
lift_gain = 6.0
edge_nodes = [0, 1, 2, 3, 12, 13, 14, 15, 0, 4, 8, 12, 3, 7, 11, 15]
opposite = [1, 0, 3, 2]

def gll_derivative():
    points = np.array([-1.0, -math.sqrt(0.2), math.sqrt(0.2), 1.0])
    table = np.zeros((4, 4))
    for i in range(4):
        for m in range(4):
            if i == m:
                total = 0.0
                for r in range(4):
                    if r != i:
                        total = total + 1.0 / (points[i] - points[r])
                table[i, m] = total
            else:
                upper = 1.0
                for r in range(4):
                    if r != i and r != m:
                        upper = upper * (points[i] - points[r])
                lower = 1.0
                for r in range(4):
                    if r != m:
                        lower = lower * (points[m] - points[r])
                table[i, m] = upper / lower
    return table

def node_tables():
    deriv_table = gll_derivative()
    along_first = np.kron(deriv_table, np.eye(4))
    along_second = np.kron(np.eye(4), deriv_table)
    lift_table = np.zeros((16, 16))
    for slot_index in range(16):
        lift_table[edge_nodes[slot_index], slot_index] = lift_gain
    return (along_first, along_second, lift_table)

def tendency(current, velocity, traces, across):
    along_first, along_second, lift_table = node_tables()
    value_type = current.dtype
    first_grad = jnp.einsum('nm,mle->nle', jnp.asarray(along_first, value_type), current, precision=lax.Precision.HIGHEST)
    second_grad = jnp.einsum('nm,mle->nle', jnp.asarray(along_second, value_type), current, precision=lax.Precision.HIGHEST)
    lifted = jnp.einsum('nt,tle->nle', jnp.asarray(lift_table, value_type), across - traces, precision=lax.Precision.HIGHEST)
    return lifted - (velocity[0] * first_grad + velocity[1] * second_grad)

def neighbor_traces(traces, index_table):
    pieces_list = []
    for side_index in range(4):
        facing = traces[4 * opposite[side_index]:4 * opposite[side_index] + 4]
        pieces_list.append(jnp.take(facing, index_table[side_index], axis=2))
    return jnp.concatenate(pieces_list, axis=0)

def matmul_rows(rows_in, weight):
    return jnp.dot(rows_in, weight, preferred_element_type=jnp.float32)

def silu_round(total):
    return jax.nn.silu(total).astype(jnp.bfloat16)

def reference(fields, velocity, neighbors, column_slot, surface, w_profile, w_surface, b_first, w_second, b_second, w_third, b_third, w_out, b_out):
    current = fields
    for section_index in range(STEPS):
        traces = current[np.array(edge_nodes)]
        across = neighbor_traces(traces, neighbors)
        current = current + step_size * tendency(current, velocity, traces, across)
    profile = jnp.transpose(fields, (2, 0, 1)).reshape(COLUMNS, LEV).astype(jnp.bfloat16)
    slot_flat = jnp.transpose(column_slot).reshape(COLUMNS)
    relaid = jnp.zeros((COLUMNS, LEV), jnp.bfloat16).at[slot_flat].set(profile)
    surface_rows = jnp.transpose(surface)
    block_rows = 2 * COLS_DEV
    blocks = (relaid.reshape(COLUMNS // block_rows, block_rows, LEV), surface_rows.reshape(COLUMNS // block_rows, block_rows, NAUX))

    def one_block(block_pair):
        layer_one = silu_round(matmul_rows(block_pair[0], w_profile) + matmul_rows(block_pair[1], w_surface) + b_first)
        layer_two = silu_round(matmul_rows(layer_one, w_second) + b_second)
        layer_three = silu_round(matmul_rows(layer_two, w_third) + b_third)
        return (matmul_rows(layer_three, w_out) + b_out).astype(jnp.bfloat16)
    tend_rows = lax.map(one_block, blocks).reshape(COLUMNS, LEV)
    heating = jnp.transpose(tend_rows[slot_flat].reshape(ELEMENTS, NODES, LEV), (1, 2, 0))
    return (current + heating.astype(jnp.float32), heating)
```

```python
import functools
import math

import jax
import jax.numpy as jnp
import numpy as np
from jax import lax
from jax.experimental import pallas as pl
from jax.experimental.pallas import tpu as pltpu
from jax.sharding import PartitionSpec as P

NODES = 16
LEV = 72
STEPS = 4
LANES = 128
STEP_SIZE = 0.05
LIFT = 6.0
EDGES = ((0, 1, 2, 3), (12, 13, 14, 15), (0, 4, 8, 12), (3, 7, 11, 15))
OPPOSITE = (1, 0, 3, 2)
NET_LIMIT = 117 << 19
ADVANCE_LIMIT = 36 << 20
HALO_ROWS = 3 * NODES * LEV + 16
BF16 = jnp.bfloat16
F32 = jnp.float32


def gll_derivative():
    points = np.array([-1.0, -math.sqrt(0.2), math.sqrt(0.2), 1.0])
    table = np.zeros((4, 4))
    for i in range(4):
        for m in range(4):
            if i == m:
                table[i, m] = sum(1.0 / (points[i] - points[r]) for r in range(4) if r != i)
            else:
                upper, lower = 1.0, 1.0
                for r in range(4):
                    if r != i and r != m:
                        upper = upper * (points[i] - points[r])
                    if r != m:
                        lower = lower * (points[m] - points[r])
                table[i, m] = upper / lower
    return table


DERIV = gll_derivative()


def low_half(rows):
    return lax.broadcasted_iota(jnp.int32, (rows, LANES), 1) < 64


def pack_surface(surface_ref, out_ref, token_ref, columns_ref, sems):
    token_ref[...] = jnp.zeros((8, LANES), F32)
    cols_dev = columns_ref.shape[1]
    start = pl.multiple_of(lax.axis_index("grp") * cols_dev, cols_dev)
    chunk = cols_dev // 4
    copies = []
    for part in range(4):
        copies.append(
            pltpu.make_async_copy(
                surface_ref.at[:, pl.ds(start + chunk * part, chunk)],
                columns_ref.at[:, chunk * part : chunk * part + chunk],
                sems.at[part],
            )
        )
        copies[-1].start()
    low = low_half(8)
    for part in range(4):
        copies[part].wait()
        for pair in range(chunk // LANES * part, chunk // LANES * (part + 1)):
            tile = columns_ref[:, LANES * pair : LANES * pair + LANES].astype(F32)
            upper, lower = tile[0:8], tile[8:16]
            out_ref[2 * pair] = jnp.where(low, upper, pltpu.roll(lower, 64, 1))
            out_ref[2 * pair + 1] = jnp.where(low, pltpu.roll(upper, 64, 1), lower)


def pack_halo(
    total,
    token_ref,
    fields_hbm,
    velocity_hbm,
    neighbors_hbm,
    near_ref,
    far_ref,
    fields_ref,
    velocity_ref,
    neighbors_ref,
    sems,
):
    del token_ref
    rows = NODES * LEV
    copies = [
        pltpu.make_async_copy(neighbors_hbm, neighbors_ref, sems.at[0]),
        pltpu.make_async_copy(fields_hbm, fields_ref, sems.at[1]),
        pltpu.make_async_copy(velocity_hbm.at[0], velocity_ref.at[0], sems.at[2]),
        pltpu.make_async_copy(velocity_hbm.at[1], velocity_ref.at[1], sems.at[3]),
    ]
    for copy in copies:
        copy.start()
    group = lax.axis_index("grp")
    first = (2 * lax.axis_index("dyn") + group) * fields_ref.shape[2]

    def fill(pairs):
        copies[0].wait()
        for out_ref, tile in pairs:
            lanes = slice(LANES * tile, LANES * tile + LANES)
            element = first + LANES * tile + lax.broadcasted_iota(jnp.int32, (4, LANES), 1)
            distance = neighbors_ref[:, lanes] - element
            distance = ((distance + total // 2) & (total - 1)) - total // 2
            padded = jnp.concatenate([distance.astype(F32), jnp.zeros((12, LANES), F32)], axis=0)
            out_ref[3 * rows : HALO_ROWS, :] = padded.astype(BF16)
        copies[1].wait()
        for out_ref, tile in pairs:
            lanes = slice(LANES * tile, LANES * tile + LANES)
            out_ref[0:rows, :] = fields_ref[:, :, lanes].reshape(rows, LANES).astype(BF16)
        for wind in range(2):
            copies[2 + wind].wait()
            for out_ref, tile in pairs:
                lanes = slice(LANES * tile, LANES * tile + LANES)
                out_ref[rows * (1 + wind) : rows * (2 + wind), :] = (
                    velocity_ref[wind, :, :, lanes].reshape(rows, LANES).astype(BF16)
                )

    @pl.when(group == 0)
    def _():
        fill([(far_ref, 0), (near_ref, 1)])

    @pl.when(group != 0)
    def _():
        fill([(far_ref, 1), (near_ref, 0)])


def silu_half(half):
    return (half + half * jnp.tanh(half)).astype(BF16)


def column_network(*refs):
    arrived_ref = refs[0]
    operands = refs[1:12]
    out_ref = refs[12]
    (
        w_profile_ref,
        w_surface_ref,
        slot_ref,
        fields_ref,
        b_first_ref,
        w_second_ref,
        b_second_ref,
        w_third_ref,
        b_third_ref,
        w_out_ref,
        b_out_ref,
    ) = refs[13:24]
    table_ref, input_ref, w_first_ref, sems = refs[24:]
    copies = [
        pltpu.make_async_copy(source, target, sems.at[i])
        for i, (source, target) in enumerate(zip(operands, refs[13:24]))
    ]
    for copy in copies:
        copy.start()
    low = low_half(8)
    for high in range(16):
        a, b, c, d = [arrived_ref[4 * high + r] for r in range(4)]
        upper = [jnp.where(low, a, pltpu.roll(b, 64, 1)), jnp.where(low, c, pltpu.roll(d, 64, 1))]
        lower = [jnp.where(low, pltpu.roll(a, 64, 1), b), jnp.where(low, pltpu.roll(c, 64, 1), d)]
        tile = jnp.concatenate(
            [jnp.concatenate(upper, axis=1), jnp.concatenate(lower, axis=1)], axis=0
        )
        table_ref[16 * high : 16 * high + 16, :] = tile.astype(BF16)
    copies[0].wait()
    copies[1].wait()
    hidden = w_first_ref.shape[1]
    w_first_ref[...] = jnp.concatenate(
        [
            w_profile_ref[...].astype(F32),
            w_surface_ref[...].astype(F32),
            jnp.zeros((8, hidden), F32),
        ],
        axis=0,
    ).astype(BF16)

    def prepare(node, place):
        slot = slot_ref[pl.ds(node, 1), :]
        placed = (slot >> 13) * 64 + (slot & 63)
        within = placed & 255
        high = placed >> 8
        rows = lax.broadcasted_iota(jnp.int32, (256, 256), 0)
        chosen = jnp.where(rows == within, 1.0, 0.0).astype(BF16)
        spread = jnp.dot(table_ref[...], chosen, preferred_element_type=F32)
        total = jnp.zeros((16, 256), F32)
        for h in range(16):
            total = total + jnp.where(high == h, spread[16 * h : 16 * h + 16, :], 0.0)
        column = jnp.concatenate([fields_ref[node], total, jnp.zeros((8, 256), F32)], axis=0)
        input_ref[place, 256 * (node % 4) : 256 * (node % 4) + 256, :] = (
            jnp.transpose(column).astype(BF16) * BF16(0.5)
        )

    def layer(value, w_ref, b_ref):
        return silu_half(
            jnp.dot(value, w_ref[...], preferred_element_type=F32) + 0.5 * b_ref[...]
        )

    for copy in copies[2:5]:
        copy.wait()
    for j in range(4):
        prepare(j, 0)
    for block in range(4):
        def ahead(j):
            if block < 3:
                prepare(4 * block + 4 + j, (block + 1) % 2)

        value = layer(input_ref[block % 2], w_first_ref, b_first_ref) * BF16(0.5)
        if block == 0:
            copies[5].wait()
            copies[6].wait()
        ahead(0)
        ahead(1)
        value = layer(value, w_second_ref, b_second_ref) * BF16(0.5)
        if block == 0:
            for copy in copies[7:11]:
                copy.wait()
            diagonal = lax.broadcasted_iota(jnp.int32, (LEV, LEV), 0) == lax.broadcasted_iota(
                jnp.int32, (LEV, LEV), 1
            )
            b_out = jnp.sum(jnp.where(diagonal, b_out_ref[...], 0.0), axis=1, keepdims=True)
        ahead(2)
        ahead(3)
        value = layer(value, w_third_ref, b_third_ref)
        result = lax.dot_general(
            w_out_ref[...], value, (((1,), (1,)), ((), ())), preferred_element_type=F32
        )
        result = result + b_out
        for j in range(4):
            out_ref[4 * block + j] = result[:, 256 * j : 256 * j + 256].astype(BF16)


class Dynamics:
    def __init__(self, total, refs):
        (
            self.current,
            self.velocity,
            self.neighbors,
            self.near,
            self.far,
            self.wind,
            self.chosen,
            self.across,
        ) = refs
        self.total = total

    def mix(self, start, count):
        low = low_half(count)
        group = lax.axis_index("grp")
        mask = jnp.logical_xor(low, jnp.broadcast_to(group, (count, LANES)) != 0)
        near = self.near[start : start + count, :].astype(F32)
        far = self.far[start : start + count, :].astype(F32)
        return jnp.where(mask, near, far), jnp.where(mask, far, near)

    def spread(self):
        rows = NODES * LEV
        for pair in range(8):
            nodes = slice(2 * pair, 2 * pair + 2)
            inner, outer = self.mix(144 * pair, 144)
            self.current[nodes, :, 256:384] = inner.reshape(2, LEV, LANES)
            self.current[nodes, :, 384:512] = outer.reshape(2, LEV, LANES)
            for w in range(2):
                inner, outer = self.mix(rows * (1 + w) + 144 * pair, 144)
                self.wind[w, nodes, :, 0:128] = inner.reshape(2, LEV, LANES)
                self.wind[w, nodes, :, 128:256] = outer.reshape(2, LEV, LANES)

    def choose(self):
        total = self.total
        first = (2 * lax.axis_index("dyn") + lax.axis_index("grp")) * 256
        inner, outer = self.mix(3 * NODES * LEV, 16)
        lane = lax.broadcasted_iota(jnp.int32, (4, LANES), 1)
        right = lane + 256
        left = lane - 128
        own = self.neighbors[...] - first
        own = ((own + total // 2) & (total - 1)) - total // 2
        place = jnp.concatenate(
            [
                own,
                jnp.where(lane < 64, right, left) + inner[0:4].astype(jnp.int32),
                jnp.where(lane < 64, left, right) + outer[0:4].astype(jnp.int32),
            ],
            axis=1,
        )
        place = jnp.where(
            place < -64,
            place + 512,
            jnp.where(place < 0, place + 384, jnp.where(place >= 320, place + 128, place)),
        )
        source = lax.broadcasted_iota(jnp.int32, (512, 512), 0)
        for k in range(4):
            self.chosen[k] = jnp.where(source == place[k : k + 1, :], 1.0, 0.0).astype(BF16)

    def move(self, tiles_in, tiles_out):
        width_in, width_out = LANES * tiles_in, LANES * tiles_out
        for k in range(4):
            facing = jnp.concatenate(
                [self.current[n, :, 0:width_in] for n in EDGES[OPPOSITE[k]]], axis=0
            ).astype(BF16)
            moved = jnp.dot(
                facing, self.chosen[k, 0:width_in, 0:width_out], preferred_element_type=F32
            )
            self.across[k, :, :, 0:width_out] = moved.reshape(4, LEV, width_out)

    def update(self, tiles_out):
        table = STEP_SIZE * DERIV
        gain = STEP_SIZE * LIFT

        def levels(part):
            for t in range(tiles_out):
                lanes = slice(LANES * t, LANES * t + LANES)
                value = [self.current[n, part, lanes] for n in range(NODES)]
                for n in range(NODES):
                    i, j = n // 4, n % 4
                    if t < 2:
                        winds = [self.velocity[w, n, part, lanes] for w in range(2)]
                    else:
                        shifted = slice(LANES * (t - 2), LANES * (t - 1))
                        winds = [self.wind[w, n, part, shifted] for w in range(2)]
                    along = [
                        [(table[i, m], value[4 * m + j]) for m in range(4)],
                        [(table[j, m], value[4 * i + m]) for m in range(4)],
                    ]
                    slopes = []
                    for terms in along:
                        kept = [float(f) * v for f, v in terms if abs(f) > 1e-12]
                        slopes.append(functools.reduce(lambda p, q: p + q, kept))
                    sides = [
                        self.across[k, EDGES[k].index(n), part, lanes]
                        for k in range(4)
                        if n in EDGES[k]
                    ]
                    new = value[n] - (winds[0] * slopes[0] + winds[1] * slopes[1])
                    if sides:
                        gathered = functools.reduce(lambda p, q: p + q, sides)
                        new = new + gain * (gathered - float(len(sides)) * value[n])
                    self.current[n, part, lanes] = new

        for index in range(LEV // 8):
            levels(slice(8 * index, 8 * index + 8))


def advance(
    total,
    fields_hbm,
    velocity_hbm,
    neighbors_hbm,
    near_ref,
    far_ref,
    heating_hbm,
    out_ref,
    current_ref,
    velocity_ref,
    neighbors_ref,
    wind_ref,
    chosen_ref,
    across_ref,
    heating_ref,
    sems,
):
    copies = [
        pltpu.make_async_copy(neighbors_hbm, neighbors_ref, sems.at[0]),
        pltpu.make_async_copy(fields_hbm, current_ref.at[:, :, 0:256], sems.at[1]),
        pltpu.make_async_copy(velocity_hbm, velocity_ref, sems.at[2]),
        pltpu.make_async_copy(heating_hbm, heating_ref, sems.at[3]),
    ]
    for copy in copies:
        copy.start()
    dynamics = Dynamics(
        total,
        (
            current_ref,
            velocity_ref,
            neighbors_ref,
            near_ref,
            far_ref,
            wind_ref,
            chosen_ref,
            across_ref,
        ),
    )
    copies[0].wait()
    dynamics.choose()
    dynamics.spread()
    copies[1].wait()
    for tiles_in, tiles_out in ((4, 4), (4, 3), (3, 3), (3, 2)):
        dynamics.move(tiles_in, tiles_out)
        if tiles_in == 4 and tiles_out == 4:
            copies[2].wait()
        dynamics.update(tiles_out)
    copies[3].wait()
    for n in range(NODES):
        out_ref[n] = current_ref[n, :, 0:256] + heating_ref[n].astype(F32)


def per_device(
    fields,
    velocity,
    neighbors,
    column_slot,
    surface,
    w_profile,
    w_surface,
    b_first,
    w_second,
    b_second,
    w_third,
    b_third,
    w_out,
    b_out,
):
    elem_dev = fields.shape[2]
    devices = lax.axis_size(("dyn", "grp"))
    chips = lax.axis_size("dyn")
    total = elem_dev * devices
    vmem = pl.BlockSpec(memory_space=pltpu.VMEM)
    hbm = pl.BlockSpec(memory_space=pl.ANY)
    cols_dev = NODES * elem_dev
    packed, token = pl.pallas_call(
        pack_surface,
        out_shape=[
            jax.ShapeDtypeStruct((chips, 8, LANES), F32),
            jax.ShapeDtypeStruct((8, LANES), F32),
        ],
        in_specs=[hbm],
        out_specs=[vmem, vmem],
        scratch_shapes=[pltpu.VMEM((16, cols_dev), BF16), pltpu.SemaphoreType.DMA((4,))],
        name="pack_surface",
    )(surface)
    arrived = lax.all_to_all(packed, "dyn", split_axis=0, concat_axis=0, tiled=True)
    near, far = pl.pallas_call(
        functools.partial(pack_halo, total),
        out_shape=[jax.ShapeDtypeStruct((HALO_ROWS, LANES), BF16)] * 2,
        in_specs=[hbm] * 4,
        out_specs=[vmem, vmem],
        scratch_shapes=[
            pltpu.VMEM(fields.shape, F32),
            pltpu.VMEM(velocity.shape, F32),
            pltpu.VMEM(neighbors.shape, jnp.int32),
            pltpu.SemaphoreType.DMA((4,)),
        ],
        compiler_params=pltpu.CompilerParams(vmem_limit_bytes=58 << 20),
        cost_estimate=pl.CostEstimate(flops=10**6, bytes_accessed=7 * 10**6, transcendentals=0),
        name="pack_halo",
    )(token, fields, velocity, neighbors)
    near = lax.ppermute(near, ("dyn", "grp"), [(i, i ^ 1) for i in range(devices)])
    far = lax.ppermute(
        far, ("dyn", "grp"), [(i, (((i + 1) ^ 1) - 1) % devices) for i in range(devices)]
    )
    operands = [
        w_profile,
        w_surface,
        column_slot,
        fields,
        b_first[None, :],
        w_second,
        b_second[None, :],
        w_third,
        b_third[None, :],
        jnp.transpose(w_out),
        b_out[None, :],
    ]
    heating = pl.pallas_call(
        column_network,
        out_shape=jax.ShapeDtypeStruct((NODES, LEV, elem_dev), BF16),
        in_specs=[vmem] + [hbm] * len(operands),
        out_specs=vmem,
        scratch_shapes=[pltpu.VMEM(x.shape, x.dtype) for x in operands]
        + [
            pltpu.VMEM((256, 256), BF16),
            pltpu.VMEM((2, 1024, 96), BF16),
            pltpu.VMEM((96, w_second.shape[0]), BF16),
            pltpu.SemaphoreType.DMA((len(operands),)),
        ],
        compiler_params=pltpu.CompilerParams(vmem_limit_bytes=NET_LIMIT),
        cost_estimate=pl.CostEstimate(
            flops=22 * 10**9, bytes_accessed=8 * 10**6, transcendentals=12 * 10**6
        ),
        name="column_network",
    )(arrived, *operands)
    advanced = pl.pallas_call(
        functools.partial(advance, total),
        out_shape=jax.ShapeDtypeStruct((NODES, LEV, elem_dev), F32),
        in_specs=[hbm, hbm, hbm, vmem, vmem, hbm],
        out_specs=vmem,
        scratch_shapes=[
            pltpu.VMEM((NODES, LEV, 512), F32),
            pltpu.VMEM(velocity.shape, F32),
            pltpu.VMEM(neighbors.shape, jnp.int32),
            pltpu.VMEM((2, NODES, LEV, 256), F32),
            pltpu.VMEM((4, 512, 512), BF16),
            pltpu.VMEM((4, 4, LEV, 512), F32),
            pltpu.VMEM((NODES, LEV, elem_dev), BF16),
            pltpu.SemaphoreType.DMA((4,)),
        ],
        compiler_params=pltpu.CompilerParams(vmem_limit_bytes=ADVANCE_LIMIT),
        cost_estimate=pl.CostEstimate(
            flops=2 * 10**9, bytes_accessed=10 * 10**6, transcendentals=0
        ),
        name="advance",
    )(fields, velocity, neighbors, near, far, heating)
    return (advanced, heating)


def solution(mesh):
    sharded = ("dyn", "grp")
    in_specs = (
        P(None, None, sharded),
        P(None, None, None, sharded),
        P(None, sharded),
        P(None, sharded),
        P(None, "dyn"),
    ) + (P(),) * 9
    out_specs = (P(None, None, sharded), P(None, None, sharded))
    return jax.shard_map(
        per_device, mesh=mesh, in_specs=in_specs, out_specs=out_specs, check_vma=False
    )
```

```python
import functools
import math

import jax
import jax.numpy as jnp
import numpy as np
from jax import lax
from jax.experimental import pallas as pl
from jax.experimental.pallas import tpu as pltpu
from jax.sharding import PartitionSpec as P

NODES = 16
LEV = 72
STEPS = 4
LANES = 128
STEP_SIZE = 0.05
LIFT = 6.0
EDGES = ((0, 1, 2, 3), (12, 13, 14, 15), (0, 4, 8, 12), (3, 7, 11, 15))
OPPOSITE = (1, 0, 3, 2)
NET_LIMIT = 117 << 19
ADVANCE_LIMIT = 36 << 20
HALO_ROWS = 3 * NODES * LEV + 16
BF16 = jnp.bfloat16
F32 = jnp.float32


def gll_derivative():
    points = np.array([-1.0, -math.sqrt(0.2), math.sqrt(0.2), 1.0])
    table = np.zeros((4, 4))
    for i in range(4):
        for m in range(4):
            if i == m:
                table[i, m] = sum(1.0 / (points[i] - points[r]) for r in range(4) if r != i)
            else:
                upper, lower = 1.0, 1.0
                for r in range(4):
                    if r != i and r != m:
                        upper = upper * (points[i] - points[r])
                    if r != m:
                        lower = lower * (points[m] - points[r])
                table[i, m] = upper / lower
    return table


DERIV = gll_derivative()


def low_half(rows):
    return lax.broadcasted_iota(jnp.int32, (rows, LANES), 1) < 64


def pack_surface(surface_ref, out_ref, token_ref, columns_ref, sems):
    token_ref[...] = jnp.zeros((8, LANES), F32)
    cols_dev = columns_ref.shape[1]
    start = pl.multiple_of(lax.axis_index("grp") * cols_dev, cols_dev)
    copy = pltpu.make_async_copy(
        surface_ref.at[:, pl.ds(start, cols_dev)], columns_ref, sems.at[0]
    )
    copy.start()
    copy.wait()
    low = low_half(8)
    for pair in range(cols_dev // LANES):
        tile = columns_ref[:, LANES * pair : LANES * pair + LANES].astype(F32)
        upper, lower = tile[0:8], tile[8:16]
        even = jnp.where(low, upper, pltpu.roll(lower, 64, 1))
        odd = jnp.where(low, pltpu.roll(upper, 64, 1), lower)
        out_ref[2 * pair] = even.astype(BF16)
        out_ref[2 * pair + 1] = odd.astype(BF16)


def pack_halo(
    total,
    token_ref,
    fields_hbm,
    velocity_hbm,
    neighbors_hbm,
    far_hbm,
    near_hbm,
    fields_ref,
    velocity_ref,
    neighbors_ref,
    far_ref,
    near_ref,
    sems,
    out_sems,
):
    del token_ref
    rows = NODES * LEV
    half = NODES // 2
    sources = [(fields_hbm, fields_ref)]
    for wind in range(2):
        sources.append((velocity_hbm.at[wind], velocity_ref.at[wind]))
    copies = []
    for array, (source, target) in enumerate(sources):
        for part in range(2):
            nodes = slice(half * part, half * part + half)
            copies.append(
                pltpu.make_async_copy(
                    source.at[nodes], target.at[nodes], sems.at[2 * array + part]
                )
            )
    neighbors_copy = pltpu.make_async_copy(neighbors_hbm, neighbors_ref, sems.at[6])
    for copy in copies:
        copy.start()
    neighbors_copy.start()
    group = lax.axis_index("grp")
    first = (2 * lax.axis_index("dyn") + group) * fields_ref.shape[2]

    def fill(far_tile):
        sent = []

        def send(start, count, number):
            part = slice(start, start + count)
            for side, (source, target) in enumerate(((far_ref, far_hbm), (near_ref, near_hbm))):
                copy = pltpu.make_async_copy(
                    source.at[part, :], target.at[part, :], out_sems.at[2 * number + side]
                )
                copy.start()
                sent.append(copy)

        pairs = [(far_ref, far_tile), (near_ref, 1 - far_tile)]
        for number, copy in enumerate(copies):
            copy.wait()
            array, part = number // 2, number % 2
            nodes = slice(half * part, half * part + half)
            start, count = rows * array + half * LEV * part, half * LEV
            for out_ref, tile in pairs:
                lanes = slice(LANES * tile, LANES * tile + LANES)
                value = sources[array][1][nodes, :, lanes]
                out_ref[start : start + count, :] = value.reshape(count, LANES).astype(BF16)
            if number == 5:
                neighbors_copy.wait()
                for out_ref, tile in pairs:
                    lanes = slice(LANES * tile, LANES * tile + LANES)
                    element = first + LANES * tile
                    element = element + lax.broadcasted_iota(jnp.int32, (4, LANES), 1)
                    distance = neighbors_ref[:, lanes] - element
                    distance = ((distance + total // 2) & (total - 1)) - total // 2
                    padded = [distance.astype(F32), jnp.zeros((12, LANES), F32)]
                    padded = jnp.concatenate(padded, axis=0)
                    out_ref[3 * rows : HALO_ROWS, :] = padded.astype(BF16)
                count = count + HALO_ROWS - 3 * rows
            send(start, count, number)
        for copy in sent:
            copy.wait()

    @pl.when(group == 0)
    def _():
        fill(0)

    @pl.when(group != 0)
    def _():
        fill(1)


def silu_half(half):
    return (half + half * jnp.tanh(half)).astype(BF16)


def column_network(*refs):
    operands = refs[:12]
    out_ref = refs[12]
    (
        arrived_ref,
        w_profile_ref,
        w_surface_ref,
        slot_ref,
        fields_ref,
        b_first_ref,
        w_second_ref,
        b_second_ref,
        w_third_ref,
        b_third_ref,
        w_out_ref,
        b_out_ref,
    ) = refs[13:25]
    table_ref, input_ref, w_first_ref, sems = refs[25:]
    sources, targets = list(operands), list(refs[13:25])
    sources[4], targets[4] = operands[4].at[0:4], fields_ref.at[0:4]
    sources.append(operands[4].at[4:NODES])
    targets.append(fields_ref.at[4:NODES])
    copies = [
        pltpu.make_async_copy(source, target, sems.at[i])
        for i, (source, target) in enumerate(zip(sources, targets))
    ]
    for copy in copies:
        copy.start()
    copies[0].wait()
    low = low_half(8)
    for high in range(16):
        a, b, c, d = [arrived_ref[4 * high + r].astype(F32) for r in range(4)]
        upper = [jnp.where(low, a, pltpu.roll(b, 64, 1)), jnp.where(low, c, pltpu.roll(d, 64, 1))]
        lower = [jnp.where(low, pltpu.roll(a, 64, 1), b), jnp.where(low, pltpu.roll(c, 64, 1), d)]
        tile = jnp.concatenate(
            [jnp.concatenate(upper, axis=1), jnp.concatenate(lower, axis=1)], axis=0
        )
        table_ref[16 * high : 16 * high + 16, :] = tile.astype(BF16)
    copies[1].wait()
    copies[2].wait()
    hidden = w_first_ref.shape[1]
    w_first_ref[...] = jnp.concatenate(
        [
            w_profile_ref[...].astype(F32),
            w_surface_ref[...].astype(F32),
            jnp.zeros((8, hidden), F32),
        ],
        axis=0,
    ).astype(BF16)

    def prepare(node, place):
        slot = slot_ref[pl.ds(node, 1), :]
        placed = (slot >> 13) * 64 + (slot & 63)
        within = placed & 255
        high = placed >> 8
        rows = lax.broadcasted_iota(jnp.int32, (256, 256), 0)
        chosen = jnp.where(rows == within, 1.0, 0.0).astype(BF16)
        spread = jnp.dot(table_ref[...], chosen, preferred_element_type=F32)
        total = jnp.zeros((16, 256), F32)
        for h in range(16):
            total = total + jnp.where(high == h, spread[16 * h : 16 * h + 16, :], 0.0)
        column = jnp.concatenate([fields_ref[node], total, jnp.zeros((8, 256), F32)], axis=0)
        input_ref[place, 256 * (node % 4) : 256 * (node % 4) + 256, :] = (
            jnp.transpose(column).astype(BF16) * BF16(0.5)
        )

    def layer(value, w_ref, b_ref):
        return silu_half(
            jnp.dot(value, w_ref[...], preferred_element_type=F32) + 0.5 * b_ref[...]
        )

    for copy in copies[3:5]:
        copy.wait()
    for j in range(4):
        prepare(j, 0)
    for block in range(4):
        def ahead(j):
            if block < 3:
                prepare(4 * block + 4 + j, (block + 1) % 2)

        if block == 0:
            copies[5].wait()
        value = layer(input_ref[block % 2], w_first_ref, b_first_ref) * BF16(0.5)
        if block == 0:
            copies[6].wait()
            copies[7].wait()
            copies[12].wait()
        ahead(0)
        ahead(1)
        value = layer(value, w_second_ref, b_second_ref) * BF16(0.5)
        if block == 0:
            for copy in copies[8:12]:
                copy.wait()
            diagonal = lax.broadcasted_iota(jnp.int32, (LEV, LEV), 0) == lax.broadcasted_iota(
                jnp.int32, (LEV, LEV), 1
            )
            b_out = jnp.sum(jnp.where(diagonal, b_out_ref[...], 0.0), axis=1, keepdims=True)
        ahead(2)
        ahead(3)
        value = layer(value, w_third_ref, b_third_ref)
        result = lax.dot_general(
            w_out_ref[...], value, (((1,), (1,)), ((), ())), preferred_element_type=F32
        )
        result = result + b_out
        for j in range(4):
            out_ref[4 * block + j] = result[:, 256 * j : 256 * j + 256].astype(BF16)


class Dynamics:
    def __init__(self, total, refs):
        (
            self.current,
            self.velocity,
            self.neighbors,
            self.near,
            self.far,
            self.wind,
            self.chosen,
            self.across,
        ) = refs
        self.total = total

    def mix(self, start, count):
        low = low_half(count)
        group = lax.axis_index("grp")
        mask = jnp.logical_xor(low, jnp.broadcast_to(group, (count, LANES)) != 0)
        near = self.near[start : start + count, :].astype(F32)
        far = self.far[start : start + count, :].astype(F32)
        return jnp.where(mask, near, far), jnp.where(mask, far, near)

    def spread(self):
        rows = NODES * LEV
        for pair in range(8):
            nodes = slice(2 * pair, 2 * pair + 2)
            inner, outer = self.mix(144 * pair, 144)
            self.current[nodes, :, 256:384] = inner.reshape(2, LEV, LANES)
            self.current[nodes, :, 384:512] = outer.reshape(2, LEV, LANES)
            for w in range(2):
                inner, outer = self.mix(rows * (1 + w) + 144 * pair, 144)
                self.wind[w, nodes, :, 0:128] = inner.reshape(2, LEV, LANES)
                self.wind[w, nodes, :, 128:256] = outer.reshape(2, LEV, LANES)

    def choose(self):
        total = self.total
        first = (2 * lax.axis_index("dyn") + lax.axis_index("grp")) * 256
        inner, outer = self.mix(3 * NODES * LEV, 16)
        lane = lax.broadcasted_iota(jnp.int32, (4, LANES), 1)
        right = lane + 256
        left = lane - 128
        own = self.neighbors[...] - first
        own = ((own + total // 2) & (total - 1)) - total // 2
        place = jnp.concatenate(
            [
                own,
                jnp.where(lane < 64, right, left) + inner[0:4].astype(jnp.int32),
                jnp.where(lane < 64, left, right) + outer[0:4].astype(jnp.int32),
            ],
            axis=1,
        )
        place = jnp.where(
            place < -64,
            place + 512,
            jnp.where(place < 0, place + 384, jnp.where(place >= 320, place + 128, place)),
        )
        source = lax.broadcasted_iota(jnp.int32, (512, 512), 0)
        for k in range(4):
            self.chosen[k] = jnp.where(source == place[k : k + 1, :], 1.0, 0.0).astype(BF16)

    def move(self, tiles_in, tiles_out):
        width_in, width_out = LANES * tiles_in, LANES * tiles_out
        for k in range(4):
            facing = jnp.concatenate(
                [self.current[n, :, 0:width_in] for n in EDGES[OPPOSITE[k]]], axis=0
            ).astype(BF16)
            moved = jnp.dot(
                facing, self.chosen[k, 0:width_in, 0:width_out], preferred_element_type=F32
            )
            self.across[k, :, :, 0:width_out] = moved.reshape(4, LEV, width_out)

    def slopes(self, line):
        table = STEP_SIZE * DERIV
        sums = (line[0] + line[3], line[1] + line[2])
        differences = (line[0] - line[3], line[1] - line[2])
        out = [None] * 4
        for i in range(2):
            odd = [0.5 * float(table[i, m] - table[i, 3 - m]) for m in range(2)]
            even = [0.5 * float(table[i, m] + table[i, 3 - m]) for m in range(2)]
            p = odd[0] * differences[0] + odd[1] * differences[1]
            q = even[0] * sums[0] + even[1] * sums[1]
            out[i], out[3 - i] = p + q, p - q
        return out

    def update(self, tiles_out):
        gain = STEP_SIZE * LIFT

        def levels(part):
            for t in range(tiles_out):
                lanes = slice(LANES * t, LANES * t + LANES)
                winds, shifted = self.velocity, lanes
                if t >= 2:
                    winds, shifted = self.wind, slice(LANES * (t - 2), LANES * (t - 1))
                value = [self.current[n, part, lanes] for n in range(NODES)]
                new = [None] * NODES
                for j in range(4):
                    slopes = self.slopes([value[4 * i + j] for i in range(4)])
                    for i in range(4):
                        n = 4 * i + j
                        sides = [
                            self.across[k, EDGES[k].index(n), part, lanes]
                            for k in range(4)
                            if n in EDGES[k]
                        ]
                        new[n] = value[n] * (1.0 - gain * len(sides)) if sides else value[n]
                        if sides:
                            new[n] = new[n] + gain * functools.reduce(lambda p, q: p + q, sides)
                        new[n] = new[n] - winds[0, n, part, shifted] * slopes[i]
                for i in range(4):
                    slopes = self.slopes(value[4 * i : 4 * i + 4])
                    for j in range(4):
                        n = 4 * i + j
                        self.current[n, part, lanes] = (
                            new[n] - winds[1, n, part, shifted] * slopes[j]
                        )

        for index in range(LEV // 8):
            levels(slice(8 * index, 8 * index + 8))


def advance(
    total,
    fields_hbm,
    velocity_hbm,
    neighbors_hbm,
    far_ref,
    near_ref,
    heating_hbm,
    out_ref,
    same_heating_hbm,
    current_ref,
    velocity_ref,
    neighbors_ref,
    wind_ref,
    chosen_ref,
    across_ref,
    heating_ref,
    sems,
):
    del same_heating_hbm
    copies = [
        pltpu.make_async_copy(neighbors_hbm, neighbors_ref, sems.at[0]),
        pltpu.make_async_copy(fields_hbm, current_ref.at[:, :, 0:256], sems.at[1]),
        pltpu.make_async_copy(velocity_hbm, velocity_ref, sems.at[2]),
        pltpu.make_async_copy(heating_hbm, heating_ref, sems.at[3]),
    ]
    for copy in copies:
        copy.start()
    dynamics = Dynamics(
        total,
        (
            current_ref,
            velocity_ref,
            neighbors_ref,
            near_ref,
            far_ref,
            wind_ref,
            chosen_ref,
            across_ref,
        ),
    )
    copies[0].wait()
    dynamics.choose()
    dynamics.spread()
    copies[1].wait()
    for tiles_in, tiles_out in ((4, 4), (4, 3), (3, 3), (3, 2)):
        dynamics.move(tiles_in, tiles_out)
        if tiles_in == 4 and tiles_out == 4:
            copies[2].wait()
        dynamics.update(tiles_out)
    copies[3].wait()
    for n in range(NODES):
        out_ref[n] = current_ref[n, :, 0:256] + heating_ref[n].astype(F32)


def per_device(
    fields,
    velocity,
    neighbors,
    column_slot,
    surface,
    w_profile,
    w_surface,
    b_first,
    w_second,
    b_second,
    w_third,
    b_third,
    w_out,
    b_out,
):
    elem_dev = fields.shape[2]
    devices = lax.axis_size(("dyn", "grp"))
    chips = lax.axis_size("dyn")
    total = elem_dev * devices
    vmem = pl.BlockSpec(memory_space=pltpu.VMEM)
    hbm = pl.BlockSpec(memory_space=pl.ANY)
    cols_dev = NODES * elem_dev
    packed, token = pl.pallas_call(
        pack_surface,
        out_shape=[
            jax.ShapeDtypeStruct((chips, 8, LANES), BF16),
            jax.ShapeDtypeStruct((8, LANES), F32),
        ],
        in_specs=[hbm],
        out_specs=[vmem, vmem],
        scratch_shapes=[pltpu.VMEM((16, cols_dev), BF16), pltpu.SemaphoreType.DMA((1,))],
        name="pack_surface",
    )(surface)
    arrived = lax.all_to_all(packed, "dyn", split_axis=0, concat_axis=0, tiled=True)
    far, near = pl.pallas_call(
        functools.partial(pack_halo, total),
        out_shape=[jax.ShapeDtypeStruct((HALO_ROWS, LANES), BF16)] * 2,
        in_specs=[hbm] * 4,
        out_specs=[hbm, hbm],
        scratch_shapes=[
            pltpu.VMEM(fields.shape, F32),
            pltpu.VMEM(velocity.shape, F32),
            pltpu.VMEM(neighbors.shape, jnp.int32),
            pltpu.VMEM((HALO_ROWS, LANES), BF16),
            pltpu.VMEM((HALO_ROWS, LANES), BF16),
            pltpu.SemaphoreType.DMA((7,)),
            pltpu.SemaphoreType.DMA((12,)),
        ],
        compiler_params=pltpu.CompilerParams(vmem_limit_bytes=NET_LIMIT),
        cost_estimate=pl.CostEstimate(flops=10**6, bytes_accessed=7 * 10**6, transcendentals=0),
        name="pack_halo",
    )(token, fields, velocity, neighbors)
    near = lax.ppermute(near, ("dyn", "grp"), [(i, i ^ 1) for i in range(devices)])
    far = lax.ppermute(
        far, ("dyn", "grp"), [(i, (((i + 1) ^ 1) - 1) % devices) for i in range(devices)]
    )
    operands = [
        arrived,
        w_profile,
        w_surface,
        column_slot,
        fields,
        b_first[None, :],
        w_second,
        b_second[None, :],
        w_third,
        b_third[None, :],
        jnp.transpose(w_out),
        b_out[None, :],
    ]
    heating = pl.pallas_call(
        column_network,
        out_shape=jax.ShapeDtypeStruct((NODES, LEV, elem_dev), BF16),
        in_specs=[hbm] * len(operands),
        out_specs=vmem,
        scratch_shapes=[pltpu.VMEM(x.shape, x.dtype) for x in operands]
        + [
            pltpu.VMEM((256, 256), BF16),
            pltpu.VMEM((2, 1024, 96), BF16),
            pltpu.VMEM((96, w_second.shape[0]), BF16),
            pltpu.SemaphoreType.DMA((len(operands) + 1,)),
        ],
        compiler_params=pltpu.CompilerParams(vmem_limit_bytes=NET_LIMIT),
        cost_estimate=pl.CostEstimate(
            flops=22 * 10**9, bytes_accessed=8 * 10**6, transcendentals=12 * 10**6
        ),
        name="column_network",
    )(*operands)
    advanced, heating = pl.pallas_call(
        functools.partial(advance, total),
        out_shape=[
            jax.ShapeDtypeStruct((NODES, LEV, elem_dev), F32),
            jax.ShapeDtypeStruct((NODES, LEV, elem_dev), BF16),
        ],
        input_output_aliases={5: 1},
        in_specs=[hbm, hbm, hbm, vmem, vmem, hbm],
        out_specs=[vmem, hbm],
        scratch_shapes=[
            pltpu.VMEM((NODES, LEV, 512), F32),
            pltpu.VMEM(velocity.shape, F32),
            pltpu.VMEM(neighbors.shape, jnp.int32),
            pltpu.VMEM((2, NODES, LEV, 256), F32),
            pltpu.VMEM((4, 512, 512), BF16),
            pltpu.VMEM((4, 4, LEV, 512), F32),
            pltpu.VMEM((NODES, LEV, elem_dev), BF16),
            pltpu.SemaphoreType.DMA((4,)),
        ],
        compiler_params=pltpu.CompilerParams(vmem_limit_bytes=ADVANCE_LIMIT),
        cost_estimate=pl.CostEstimate(
            flops=2 * 10**9, bytes_accessed=10 * 10**6, transcendentals=0
        ),
        name="advance",
    )(fields, velocity, neighbors, far, near, heating)
    return (advanced, heating)


def solution(mesh):
    sharded = ("dyn", "grp")
    in_specs = (
        P(None, None, sharded),
        P(None, None, None, sharded),
        P(None, sharded),
        P(None, sharded),
        P(None, "dyn"),
    ) + (P(),) * 9
    out_specs = (P(None, None, sharded), P(None, None, sharded))
    return jax.shard_map(
        per_device, mesh=mesh, in_specs=in_specs, out_specs=out_specs, check_vma=False
    )
```

```python
import functools
import math

import jax
import jax.numpy as jnp
import numpy as np
from jax import lax
from jax.experimental import pallas as pl
from jax.experimental.pallas import tpu as pltpu
from jax.sharding import PartitionSpec as P

NODES = 16
LEV = 72
STEPS = 4
LANES = 128
STEP_SIZE = 0.05
LIFT = 6.0
EDGES = ((0, 1, 2, 3), (12, 13, 14, 15), (0, 4, 8, 12), (3, 7, 11, 15))
OPPOSITE = (1, 0, 3, 2)
NET_LIMIT = 117 << 19
ADVANCE_LIMIT = 36 << 20
HALO_ROWS = 3 * NODES * LEV + 16
BF16 = jnp.bfloat16
F32 = jnp.float32


def gll_derivative():
    points = np.array([-1.0, -math.sqrt(0.2), math.sqrt(0.2), 1.0])
    table = np.zeros((4, 4))
    for i in range(4):
        for m in range(4):
            if i == m:
                table[i, m] = sum(1.0 / (points[i] - points[r]) for r in range(4) if r != i)
            else:
                upper, lower = 1.0, 1.0
                for r in range(4):
                    if r != i and r != m:
                        upper = upper * (points[i] - points[r])
                    if r != m:
                        lower = lower * (points[m] - points[r])
                table[i, m] = upper / lower
    return table


DERIV = gll_derivative()


def low_half(rows):
    return lax.broadcasted_iota(jnp.int32, (rows, LANES), 1) < 64


def pack_surface(surface_ref, out_ref, token_ref, columns_ref, sems):
    token_ref[...] = jnp.zeros((8, LANES), F32)
    cols_dev = columns_ref.shape[1]
    start = pl.multiple_of(lax.axis_index("grp") * cols_dev, cols_dev)
    copy = pltpu.make_async_copy(
        surface_ref.at[:, pl.ds(start, cols_dev)], columns_ref, sems.at[0]
    )
    copy.start()
    copy.wait()
    low = low_half(8)
    for pair in range(cols_dev // LANES):
        tile = columns_ref[:, LANES * pair : LANES * pair + LANES].astype(F32)
        upper, lower = tile[0:8], tile[8:16]
        even = jnp.where(low, upper, pltpu.roll(lower, 64, 1))
        odd = jnp.where(low, pltpu.roll(upper, 64, 1), lower)
        out_ref[2 * pair] = even.astype(BF16)
        out_ref[2 * pair + 1] = odd.astype(BF16)


def pack_halo(
    total,
    token_ref,
    fields_hbm,
    velocity_hbm,
    neighbors_hbm,
    far_hbm,
    near_hbm,
    fields_ref,
    velocity_ref,
    neighbors_ref,
    far_ref,
    near_ref,
    sems,
    out_sems,
):
    del token_ref
    rows = NODES * LEV
    half = NODES // 2
    sources = [(fields_hbm, fields_ref)]
    for wind in range(2):
        sources.append((velocity_hbm.at[wind], velocity_ref.at[wind]))
    copies = []
    for array, (source, target) in enumerate(sources):
        for part in range(2):
            nodes = slice(half * part, half * part + half)
            copies.append(
                pltpu.make_async_copy(
                    source.at[nodes], target.at[nodes], sems.at[2 * array + part]
                )
            )
    neighbors_copy = pltpu.make_async_copy(neighbors_hbm, neighbors_ref, sems.at[6])
    for copy in copies:
        copy.start()
    neighbors_copy.start()
    group = lax.axis_index("grp")
    first = (2 * lax.axis_index("dyn") + group) * fields_ref.shape[2]

    def fill(far_tile):
        sent = []

        def send(start, count, number):
            part = slice(start, start + count)
            for side, (source, target) in enumerate(((far_ref, far_hbm), (near_ref, near_hbm))):
                copy = pltpu.make_async_copy(
                    source.at[part, :], target.at[part, :], out_sems.at[2 * number + side]
                )
                copy.start()
                sent.append(copy)

        pairs = [(far_ref, far_tile), (near_ref, 1 - far_tile)]
        for number, copy in enumerate(copies):
            copy.wait()
            array, part = number // 2, number % 2
            nodes = slice(half * part, half * part + half)
            start, count = rows * array + half * LEV * part, half * LEV
            for out_ref, tile in pairs:
                lanes = slice(LANES * tile, LANES * tile + LANES)
                value = sources[array][1][nodes, :, lanes]
                out_ref[start : start + count, :] = value.reshape(count, LANES).astype(BF16)
            if number == 5:
                neighbors_copy.wait()
                for out_ref, tile in pairs:
                    lanes = slice(LANES * tile, LANES * tile + LANES)
                    element = first + LANES * tile
                    element = element + lax.broadcasted_iota(jnp.int32, (4, LANES), 1)
                    distance = neighbors_ref[:, lanes] - element
                    distance = ((distance + total // 2) & (total - 1)) - total // 2
                    padded = [distance.astype(F32), jnp.zeros((12, LANES), F32)]
                    padded = jnp.concatenate(padded, axis=0)
                    out_ref[3 * rows : HALO_ROWS, :] = padded.astype(BF16)
                count = count + HALO_ROWS - 3 * rows
            send(start, count, number)
        for copy in sent:
            copy.wait()

    @pl.when(group == 0)
    def _():
        fill(0)

    @pl.when(group != 0)
    def _():
        fill(1)


def silu_half(half):
    return (half + half * jnp.tanh(half)).astype(BF16)


def column_network(*refs):
    operands = refs[:12]
    out_hbm = refs[12]
    (
        arrived_ref,
        w_profile_ref,
        w_surface_ref,
        slot_ref,
        fields_ref,
        b_first_ref,
        w_second_ref,
        b_second_ref,
        w_third_ref,
        b_third_ref,
        w_out_ref,
        b_out_ref,
    ) = refs[14:26]
    table_ref, input_ref, w_first_ref, out_ref, sems, out_sems = refs[26:]
    sources, targets = list(operands), list(refs[14:26])
    sources[4], targets[4] = operands[4].at[0:4], fields_ref.at[0:4]
    sources.append(operands[4].at[4:NODES])
    targets.append(fields_ref.at[4:NODES])
    copies = [
        pltpu.make_async_copy(source, target, sems.at[i])
        for i, (source, target) in enumerate(zip(sources, targets))
    ]
    for copy in copies:
        copy.start()
    copies[0].wait()
    low = low_half(8)
    for high in range(16):
        a, b, c, d = [arrived_ref[4 * high + r].astype(F32) for r in range(4)]
        upper = [jnp.where(low, a, pltpu.roll(b, 64, 1)), jnp.where(low, c, pltpu.roll(d, 64, 1))]
        lower = [jnp.where(low, pltpu.roll(a, 64, 1), b), jnp.where(low, pltpu.roll(c, 64, 1), d)]
        tile = jnp.concatenate(
            [jnp.concatenate(upper, axis=1), jnp.concatenate(lower, axis=1)], axis=0
        )
        table_ref[16 * high : 16 * high + 16, :] = tile.astype(BF16)
    copies[1].wait()
    copies[2].wait()
    hidden = w_first_ref.shape[1]
    w_first_ref[...] = jnp.concatenate(
        [
            w_profile_ref[...].astype(F32),
            w_surface_ref[...].astype(F32),
            jnp.zeros((8, hidden), F32),
        ],
        axis=0,
    ).astype(BF16)

    def prepare(node, place):
        slot = slot_ref[pl.ds(node, 1), :]
        placed = (slot >> 13) * 64 + (slot & 63)
        within = placed & 255
        high = placed >> 8
        rows = lax.broadcasted_iota(jnp.int32, (256, 256), 0)
        chosen = jnp.where(rows == within, 1.0, 0.0).astype(BF16)
        spread = jnp.dot(table_ref[...], chosen, preferred_element_type=F32)
        total = jnp.zeros((16, 256), F32)
        for h in range(16):
            total = total + jnp.where(high == h, spread[16 * h : 16 * h + 16, :], 0.0)
        column = jnp.concatenate([fields_ref[node], total, jnp.zeros((8, 256), F32)], axis=0)
        input_ref[place, 256 * (node % 4) : 256 * (node % 4) + 256, :] = (
            jnp.transpose(column).astype(BF16) * BF16(0.5)
        )

    def layer(value, w_ref, b_ref):
        return silu_half(
            jnp.dot(value, w_ref[...], preferred_element_type=F32) + 0.5 * b_ref[...]
        )

    for copy in copies[3:5]:
        copy.wait()
    for j in range(4):
        prepare(j, 0)
    sent = []
    for block in range(4):
        def ahead(j):
            if block < 3:
                prepare(4 * block + 4 + j, (block + 1) % 2)

        if block == 0:
            copies[5].wait()
        value = layer(input_ref[block % 2], w_first_ref, b_first_ref) * BF16(0.5)
        if block == 0:
            copies[6].wait()
            copies[7].wait()
            copies[12].wait()
        ahead(0)
        ahead(1)
        value = layer(value, w_second_ref, b_second_ref) * BF16(0.5)
        if block == 0:
            for copy in copies[8:12]:
                copy.wait()
            diagonal = lax.broadcasted_iota(jnp.int32, (LEV, LEV), 0) == lax.broadcasted_iota(
                jnp.int32, (LEV, LEV), 1
            )
            b_out = jnp.sum(jnp.where(diagonal, b_out_ref[...], 0.0), axis=1, keepdims=True)
        ahead(2)
        ahead(3)
        value = layer(value, w_third_ref, b_third_ref)
        result = lax.dot_general(
            w_out_ref[...], value, (((1,), (1,)), ((), ())), preferred_element_type=F32
        )
        result = result + b_out
        for j in range(4):
            out_ref[4 * block + j] = result[:, 256 * j : 256 * j + 256].astype(BF16)
        nodes = slice(4 * block, 4 * block + 4)
        sent.append(
            pltpu.make_async_copy(out_ref.at[nodes], out_hbm.at[nodes], out_sems.at[block])
        )
        sent[-1].start()
    for copy in sent:
        copy.wait()


class Dynamics:
    def __init__(self, total, refs):
        (
            self.current,
            self.velocity,
            self.neighbors,
            self.near,
            self.far,
            self.wind,
            self.chosen,
            self.across,
        ) = refs
        self.total = total

    def mix(self, start, count):
        low = low_half(count)
        group = lax.axis_index("grp")
        mask = jnp.logical_xor(low, jnp.broadcast_to(group, (count, LANES)) != 0)
        near = self.near[start : start + count, :].astype(F32)
        far = self.far[start : start + count, :].astype(F32)
        return jnp.where(mask, near, far), jnp.where(mask, far, near)

    def spread(self):
        rows = NODES * LEV
        for pair in range(8):
            nodes = slice(2 * pair, 2 * pair + 2)
            inner, outer = self.mix(144 * pair, 144)
            self.current[nodes, :, 256:384] = inner.reshape(2, LEV, LANES)
            self.current[nodes, :, 384:512] = outer.reshape(2, LEV, LANES)
            for w in range(2):
                inner, outer = self.mix(rows * (1 + w) + 144 * pair, 144)
                self.wind[w, nodes, :, 0:128] = inner.reshape(2, LEV, LANES)
                self.wind[w, nodes, :, 128:256] = outer.reshape(2, LEV, LANES)

    def choose(self):
        total = self.total
        first = (2 * lax.axis_index("dyn") + lax.axis_index("grp")) * 256
        inner, outer = self.mix(3 * NODES * LEV, 16)
        lane = lax.broadcasted_iota(jnp.int32, (4, LANES), 1)
        right = lane + 256
        left = lane - 128
        own = self.neighbors[...] - first
        own = ((own + total // 2) & (total - 1)) - total // 2
        place = jnp.concatenate(
            [
                own,
                jnp.where(lane < 64, right, left) + inner[0:4].astype(jnp.int32),
                jnp.where(lane < 64, left, right) + outer[0:4].astype(jnp.int32),
            ],
            axis=1,
        )
        place = jnp.where(
            place < -64,
            place + 512,
            jnp.where(place < 0, place + 384, jnp.where(place >= 320, place + 128, place)),
        )
        source = lax.broadcasted_iota(jnp.int32, (512, 512), 0)
        for k in range(4):
            self.chosen[k] = jnp.where(source == place[k : k + 1, :], 1.0, 0.0).astype(BF16)

    def move(self, tiles_in, tiles_out):
        width_in, width_out = LANES * tiles_in, LANES * tiles_out
        for k in range(4):
            facing = jnp.concatenate(
                [self.current[n, :, 0:width_in] for n in EDGES[OPPOSITE[k]]], axis=0
            ).astype(BF16)
            moved = jnp.dot(
                facing, self.chosen[k, 0:width_in, 0:width_out], preferred_element_type=F32
            )
            self.across[k, :, :, 0:width_out] = moved.reshape(4, LEV, width_out)

    def slopes(self, line):
        table = STEP_SIZE * DERIV
        sums = (line[0] + line[3], line[1] + line[2])
        differences = (line[0] - line[3], line[1] - line[2])
        out = [None] * 4
        for i in range(2):
            odd = [0.5 * float(table[i, m] - table[i, 3 - m]) for m in range(2)]
            even = [0.5 * float(table[i, m] + table[i, 3 - m]) for m in range(2)]
            p = odd[0] * differences[0] + odd[1] * differences[1]
            q = even[0] * sums[0] + even[1] * sums[1]
            out[i], out[3 - i] = p + q, p - q
        return out

    def update(self, tiles_out):
        gain = STEP_SIZE * LIFT

        def levels(part):
            for t in range(tiles_out):
                lanes = slice(LANES * t, LANES * t + LANES)
                winds, shifted = self.velocity, lanes
                if t >= 2:
                    winds, shifted = self.wind, slice(LANES * (t - 2), LANES * (t - 1))
                value = [self.current[n, part, lanes] for n in range(NODES)]
                new = [None] * NODES
                for j in range(4):
                    slopes = self.slopes([value[4 * i + j] for i in range(4)])
                    for i in range(4):
                        n = 4 * i + j
                        sides = [
                            self.across[k, EDGES[k].index(n), part, lanes]
                            for k in range(4)
                            if n in EDGES[k]
                        ]
                        new[n] = value[n] * (1.0 - gain * len(sides)) if sides else value[n]
                        if sides:
                            new[n] = new[n] + gain * functools.reduce(lambda p, q: p + q, sides)
                        new[n] = new[n] - winds[0, n, part, shifted] * slopes[i]
                for i in range(4):
                    slopes = self.slopes(value[4 * i : 4 * i + 4])
                    for j in range(4):
                        n = 4 * i + j
                        self.current[n, part, lanes] = (
                            new[n] - winds[1, n, part, shifted] * slopes[j]
                        )

        for index in range(LEV // 8):
            levels(slice(8 * index, 8 * index + 8))


def advance(
    total,
    fields_hbm,
    velocity_hbm,
    neighbors_hbm,
    far_ref,
    near_ref,
    heating_hbm,
    out_hbm,
    same_heating_hbm,
    current_ref,
    velocity_ref,
    neighbors_ref,
    wind_ref,
    chosen_ref,
    across_ref,
    heating_ref,
    out_ref,
    sems,
    out_sems,
):
    del same_heating_hbm
    copies = [
        pltpu.make_async_copy(neighbors_hbm, neighbors_ref, sems.at[0]),
        pltpu.make_async_copy(fields_hbm, current_ref.at[:, :, 0:256], sems.at[1]),
        pltpu.make_async_copy(velocity_hbm, velocity_ref, sems.at[2]),
        pltpu.make_async_copy(heating_hbm, heating_ref, sems.at[3]),
    ]
    for copy in copies:
        copy.start()
    dynamics = Dynamics(
        total,
        (
            current_ref,
            velocity_ref,
            neighbors_ref,
            near_ref,
            far_ref,
            wind_ref,
            chosen_ref,
            across_ref,
        ),
    )
    copies[0].wait()
    dynamics.choose()
    dynamics.spread()
    copies[1].wait()
    for tiles_in, tiles_out in ((4, 4), (4, 3), (3, 3), (3, 2)):
        dynamics.move(tiles_in, tiles_out)
        if tiles_in == 4 and tiles_out == 4:
            copies[2].wait()
        dynamics.update(tiles_out)
    copies[3].wait()
    sent = []
    for block in range(4):
        nodes = slice(4 * block, 4 * block + 4)
        for n in range(4 * block, 4 * block + 4):
            out_ref[n] = current_ref[n, :, 0:256] + heating_ref[n].astype(F32)
        sent.append(
            pltpu.make_async_copy(out_ref.at[nodes], out_hbm.at[nodes], out_sems.at[block])
        )
        sent[-1].start()
    for copy in sent:
        copy.wait()


def per_device(
    fields,
    velocity,
    neighbors,
    column_slot,
    surface,
    w_profile,
    w_surface,
    b_first,
    w_second,
    b_second,
    w_third,
    b_third,
    w_out,
    b_out,
):
    elem_dev = fields.shape[2]
    devices = lax.axis_size(("dyn", "grp"))
    chips = lax.axis_size("dyn")
    total = elem_dev * devices
    vmem = pl.BlockSpec(memory_space=pltpu.VMEM)
    hbm = pl.BlockSpec(memory_space=pl.ANY)
    cols_dev = NODES * elem_dev
    packed, token = pl.pallas_call(
        pack_surface,
        out_shape=[
            jax.ShapeDtypeStruct((chips, 8, LANES), BF16),
            jax.ShapeDtypeStruct((8, LANES), F32),
        ],
        in_specs=[hbm],
        out_specs=[vmem, vmem],
        scratch_shapes=[pltpu.VMEM((16, cols_dev), BF16), pltpu.SemaphoreType.DMA((1,))],
        name="pack_surface",
    )(surface)
    arrived = lax.all_to_all(packed, "dyn", split_axis=0, concat_axis=0, tiled=True)
    far, near = pl.pallas_call(
        functools.partial(pack_halo, total),
        out_shape=[jax.ShapeDtypeStruct((HALO_ROWS, LANES), BF16)] * 2,
        in_specs=[hbm] * 4,
        out_specs=[hbm, hbm],
        scratch_shapes=[
            pltpu.VMEM(fields.shape, F32),
            pltpu.VMEM(velocity.shape, F32),
            pltpu.VMEM(neighbors.shape, jnp.int32),
            pltpu.VMEM((HALO_ROWS, LANES), BF16),
            pltpu.VMEM((HALO_ROWS, LANES), BF16),
            pltpu.SemaphoreType.DMA((7,)),
            pltpu.SemaphoreType.DMA((12,)),
        ],
        compiler_params=pltpu.CompilerParams(vmem_limit_bytes=NET_LIMIT),
        cost_estimate=pl.CostEstimate(flops=10**6, bytes_accessed=7 * 10**6, transcendentals=0),
        name="pack_halo",
    )(token, fields, velocity, neighbors)
    near = lax.ppermute(near, ("dyn", "grp"), [(i, i ^ 1) for i in range(devices)])
    far = lax.ppermute(
        far, ("dyn", "grp"), [(i, (((i + 1) ^ 1) - 1) % devices) for i in range(devices)]
    )
    operands = [
        arrived,
        w_profile,
        w_surface,
        column_slot,
        fields,
        b_first[None, :],
        w_second,
        b_second[None, :],
        w_third,
        b_third[None, :],
        jnp.transpose(w_out),
        b_out[None, :],
    ]
    heating, _ = pl.pallas_call(
        column_network,
        out_shape=[
            jax.ShapeDtypeStruct((NODES, LEV, elem_dev), BF16),
            jax.ShapeDtypeStruct(arrived.shape, BF16),
        ],
        input_output_aliases={0: 1},
        in_specs=[hbm] * len(operands),
        out_specs=[hbm, hbm],
        scratch_shapes=[pltpu.VMEM(x.shape, x.dtype) for x in operands]
        + [
            pltpu.VMEM((256, 256), BF16),
            pltpu.VMEM((2, 1024, 96), BF16),
            pltpu.VMEM((96, w_second.shape[0]), BF16),
            pltpu.VMEM((NODES, LEV, elem_dev), BF16),
            pltpu.SemaphoreType.DMA((len(operands) + 1,)),
            pltpu.SemaphoreType.DMA((4,)),
        ],
        compiler_params=pltpu.CompilerParams(vmem_limit_bytes=NET_LIMIT),
        cost_estimate=pl.CostEstimate(
            flops=22 * 10**9, bytes_accessed=8 * 10**6, transcendentals=12 * 10**6
        ),
        name="column_network",
    )(*operands)
    advanced, heating = pl.pallas_call(
        functools.partial(advance, total),
        out_shape=[
            jax.ShapeDtypeStruct((NODES, LEV, elem_dev), F32),
            jax.ShapeDtypeStruct((NODES, LEV, elem_dev), BF16),
        ],
        input_output_aliases={5: 1},
        in_specs=[hbm, hbm, hbm, vmem, vmem, hbm],
        out_specs=[hbm, hbm],
        scratch_shapes=[
            pltpu.VMEM((NODES, LEV, 512), F32),
            pltpu.VMEM(velocity.shape, F32),
            pltpu.VMEM(neighbors.shape, jnp.int32),
            pltpu.VMEM((2, NODES, LEV, 256), F32),
            pltpu.VMEM((4, 512, 512), BF16),
            pltpu.VMEM((4, 4, LEV, 512), F32),
            pltpu.VMEM((NODES, LEV, elem_dev), BF16),
            pltpu.VMEM((NODES, LEV, elem_dev), F32),
            pltpu.SemaphoreType.DMA((4,)),
            pltpu.SemaphoreType.DMA((4,)),
        ],
        compiler_params=pltpu.CompilerParams(vmem_limit_bytes=ADVANCE_LIMIT),
        cost_estimate=pl.CostEstimate(
            flops=2 * 10**9, bytes_accessed=10 * 10**6, transcendentals=0
        ),
        name="advance",
    )(fields, velocity, neighbors, far, near, heating)
    return (advanced, heating)


def solution(mesh):
    sharded = ("dyn", "grp")
    in_specs = (
        P(None, None, sharded),
        P(None, None, None, sharded),
        P(None, sharded),
        P(None, sharded),
        P(None, "dyn"),
    ) + (P(),) * 9
    out_specs = (P(None, None, sharded), P(None, None, sharded))
    return jax.shard_map(
        per_device, mesh=mesh, in_specs=in_specs, out_specs=out_specs, check_vma=False
    )
```
